32 devices in a mesh: gx: 4 (over x, core), gy: 8 (over z, y).
Axes of the slice: x: 2, y: 2, z: 4, core: 2. Of those that a mesh axis runs over, the one named last changes fastest.
Arguments:
- velocity: float32 [3, 32, 32, 128], P(None, 'gx', 'gy'), may hold values from -6 to 6
- stress: float32 [6, 32, 32, 128], P(None, 'gx', 'gy'), may hold values from -6 to 6
- memory: float32 [6, 32, 32, 128], P(None, 'gx', 'gy'), may hold values from -3 to 3
- buoyancy: float32 [32, 32, 128], P('gx', 'gy'), may hold values from 0.5 to 1.5
- lame_lambda: float32 [32, 32, 128], P('gx', 'gy'), may hold values from 0.5 to 1.5
- shear_modulus: float32 [32, 32, 128], P('gx', 'gy'), may hold values from 0.3 to 1
- relaxation: float32 [32, 32, 128], P('gx', 'gy'), may hold values from 0.05 to 0.4
- surface_history: bfloat16 [32, 32, 3, 1020], P('gx', 'gy'), may hold values from -6 to 6
- site_owner: int32 [4, 8, 8, 4, 1], P('gx', 'gy'), may hold values from 0 to 7; in each aligned block of 32 rows (0 to 31, 32 to 63, ..., all dimensions but the last counted through in order) at most 8 rows name the same one
- periods: float32 [100], replicated, may hold values from 3 to 300
Outputs:
- final_velocity: float32 [3, 32, 32, 128], P(None, 'gx', 'gy')
- final_stress: float32 [6, 32, 32, 128], P(None, 'gx', 'gy')
- final_memory: float32 [6, 32, 32, 128], P(None, 'gx', 'gy')
- block_energy: float32 [4, 8, 3, 400], P('gx', 'gy')
The draws below stay inside these ranges and needn't reach their ends.
Inputs may be any that keep to these rules, and one draw needn't show every extreme that they name: `site_owner`: among the 32 sites of one device no site block is named more than 8 times, and some block is named exactly 8 times.
All inputs are finite; a program needn't handle non-finite values.
Results may differ from the reference program's by a relative error of at most 0.001.
Values may be sent and summed in bfloat16 or wider, within the bound.
A program may use at most 64 MiB of HBM per device.

```python
import math
import jax
import jax.numpy as jnp
import numpy as np
from jax import lax

CX = 8
CY = 4
CZ = 128
ITERS = 4
P_SIZE = 100
HIST = 1020
NX = 32
NY = 32
SITES = 32
CAP = 8
N_GX = 4
N_GY = 8


def level_of(own_key, extent, split, smallest, high):
    def one(axis_at, shards_of):
        draws = jax.random.uniform(jax.random.fold_in(jax.random.fold_in(own_key, 6), axis_at), (shards_of,), jnp.float32, smallest / len(split), high / len(split))
        return jnp.repeat(jnp.exp(draws), extent[axis_at] // shards_of).reshape((-1,) + (1,) * (len(extent) - axis_at - 1))

    loudness = one(*split[0])
    for cut in split[1:]:
        loudness = loudness * one(*cut)
    return loudness


def assign_block(stream_key, own, number, rows, number_of, top, bound, lean):
    sequence = jax.random.permutation(stream_key, number_of)
    packed, ordinary = load_shares(number_of, rows * top, bound, lean, True), load_shares(number_of, rows * top, bound, lean, False)
    places = jnp.arange(number_of)

    def named(lengths, turn):
        used = int((lengths > 0).sum())
        fixed = max(1, used // 4)
        moved = fixed + (places - fixed + turn * (used - fixed)) % max(1, number_of - fixed)
        return jnp.zeros((number_of,), jnp.int32).at[sequence[jnp.where(places < fixed, places, moved)]].set(jnp.asarray(lengths, jnp.int32))

    lengths = jnp.where(number % 4 == 0, named(packed, number // 4), named(ordinary, number - number // 4 - 1))
    mixed = jax.random.permutation(jax.random.fold_in(own, 3), number_of)
    donor, receiver = mixed[0:number_of // 2 * 2:2], mixed[1:number_of // 2 * 2:2]
    margin = jnp.minimum(lengths[donor] - 1, bound - lengths[receiver]) // 2
    margin = jnp.where((donor == sequence[0]) | (receiver == sequence[0]) | (lengths[receiver] == 0), 0, jnp.maximum(margin, 0))
    moved = jax.random.randint(jax.random.fold_in(own, 4), (number_of // 2,), 0, 1 << 20) % (margin + 1)
    lengths = lengths.at[donor].add(-moved).at[receiver].add(moved)
    members = jnp.searchsorted(jnp.cumsum(lengths), jnp.arange(rows * top), side="right").astype(jnp.int32)
    table = members.reshape(top, rows).T
    table = table[jax.random.permutation(jax.random.fold_in(own, 1), rows)]
    turn = jax.random.randint(jax.random.fold_in(own, 2), (rows, 1), 0, top)
    return jnp.take_along_axis(table, (jnp.arange(top)[None, :] + turn) % top, axis=1)


def load_shares(count, total, most, lean, full):
    portions = [(1 << 20) // math.isqrt(grade ** lean) + 1 for grade in range(1, count + 1)]
    largest = most if full else min(most, max(-(-total // count), total * portions[0] // sum(portions)))
    least = 1 if total - largest >= count - 1 else 0
    holding, rest = [largest] + [least] * (count - 1), total - largest - least * (count - 1)
    while rest > 0:
        free = [i for i in range(1, count) if holding[i] < largest] or [i for i in range(1, count) if holding[i] < most]
        whole, left = sum([portions[i] for i in free]), rest
        for i in free:
            more = min(most - holding[i], max(1, left * portions[i] // whole), rest)
            holding[i] = holding[i] + more
            rest = rest - more
    return np.array(holding)


def bell_draw(rng, shape, scale, most, shards=(), kind=jnp.bfloat16):
    factor_of = level_of(rng, shape, shards, -0.22, 0.18) if shards else 1.0
    values = jax.random.normal(rng, shape, jnp.float32) * scale * factor_of
    return jnp.minimum(jnp.maximum(values, -most), most).astype(kind)


def setup_inputs(seed: int = 0) -> dict:
    streams_of = jax.random.split(jax.random.key(seed), 11)
    velocity = bell_draw(streams_of[0], (3, NX, NY, CZ), 1.0, 6.0, ((1, 4), (2, 8)), jnp.float32)
    stress = bell_draw(streams_of[1], (6, NX, NY, CZ), 1.0, 6.0, ((1, 4), (2, 8)), jnp.float32)
    memory = bell_draw(streams_of[2], (6, NX, NY, CZ), 0.5, 3.0, ((1, 4), (2, 8)), jnp.float32)
    buoyancy = jnp.clip(0.5 + 1.0 * jax.random.uniform(streams_of[3], (NX, NY, CZ), jnp.float32) ** level_of(streams_of[3], (NX, NY, CZ), ((0, 4), (1, 8)), -0.2, 0.2), 0.5, 1.5)
    lame_lambda = jnp.clip(0.5 + 1.0 * jax.random.uniform(streams_of[4], (NX, NY, CZ), jnp.float32) ** level_of(streams_of[4], (NX, NY, CZ), ((0, 4), (1, 8)), -0.2, 0.2), 0.5, 1.5)
    shear_modulus = jnp.clip(0.3 + 0.7 * jax.random.uniform(streams_of[5], (NX, NY, CZ), jnp.float32) ** level_of(streams_of[5], (NX, NY, CZ), ((0, 4), (1, 8)), -0.2, 0.2), 0.3, 1.0)
    relaxation = jnp.clip(0.05 + 0.35 * jax.random.uniform(streams_of[6], (NX, NY, CZ), jnp.float32) ** level_of(streams_of[6], (NX, NY, CZ), ((0, 4), (1, 8)), -0.2, 0.2), 0.05, 0.4)
    surface_history = bell_draw(streams_of[7], (NX, NY, 3, HIST), 1.0, 6.0, ((0, 4), (1, 8)))
    site_owner_keys = jax.random.split(jax.random.fold_in(streams_of[8], 1), N_GX * N_GY * CX * CY // SITES)
    site_owner_turns = jax.random.permutation(jax.random.fold_in(streams_of[8], 3), N_GX * N_GY * CX * CY // SITES)
    site_owner = jax.vmap(lambda own, number: assign_block(jax.random.fold_in(streams_of[8], 2), own, number, SITES, N_GY, 1, CAP, 2))(site_owner_keys, site_owner_turns).reshape((N_GX, N_GY, CX, CY, 1))
    periods = jnp.clip(jnp.exp(jax.random.uniform(streams_of[9], (P_SIZE,), jnp.float32, math.log(3.0), math.log(300.0))), 3.0, 300.0)
    return dict(velocity=velocity, stress=stress, memory=memory, buoyancy=buoyancy, lame_lambda=lame_lambda, shear_modulus=shear_modulus, relaxation=relaxation, surface_history=surface_history, site_owner=site_owner, periods=periods)


TIME_STEP = 0.25
DAMPING = 0.05
RELAX = math.exp(-0.25 / 8.0)

def central(field, axis):
    count = field.shape[axis]
    widths = [(0, 0)] * field.ndim
    widths[axis] = (1, 1)
    padded = jnp.pad(field, widths)
    upper = lax.slice_in_dim(padded, 2, count + 2, axis=axis)
    lower = lax.slice_in_dim(padded, 0, count, axis=axis)
    return 0.5 * (upper - lower)

def oscillator_table(periods, hist, iters):
    count_periods = periods.shape[0]
    span = iters * count_periods
    omega = (2.0 * math.pi / jnp.tile(periods, iters))[None, :]
    damped = omega * math.sqrt(1.0 - DAMPING * DAMPING)
    width = hist + iters
    rows = jnp.arange(width, dtype=jnp.int32)[:, None]
    step_of = (jnp.arange(span, dtype=jnp.int32) // count_periods)[None, :]
    lag = hist + step_of - rows
    valid = (lag >= 0) & (lag <= hist)
    lagf = jnp.clip(lag, 0, hist).astype(jnp.float32)
    value = omega * jnp.exp(-DAMPING * omega * lagf) * jnp.sin(damped * lagf) / damped
    return jnp.where(valid, value, 0.0).astype(jnp.bfloat16)

def wave_step(velocity, stress, memory, buoyancy, lame_lambda, shear_modulus, relaxation):
    force_x = central(stress[0], 0) + central(stress[3], 1) + central(stress[4], 2)
    force_y = central(stress[3], 0) + central(stress[1], 1) + central(stress[5], 2)
    force_z = central(stress[4], 0) + central(stress[5], 1) + central(stress[2], 2)
    velocity = velocity + TIME_STEP * buoyancy * jnp.stack([force_x, force_y, force_z])
    strain_xx = central(velocity[0], 0)
    strain_yy = central(velocity[1], 1)
    strain_zz = central(velocity[2], 2)
    strain_xy = 0.5 * (central(velocity[0], 1) + central(velocity[1], 0))
    strain_xz = 0.5 * (central(velocity[0], 2) + central(velocity[2], 0))
    strain_yz = 0.5 * (central(velocity[1], 2) + central(velocity[2], 1))
    trace = strain_xx + strain_yy + strain_zz
    elastic = jnp.stack([lame_lambda * trace + 2.0 * shear_modulus * strain_xx, lame_lambda * trace + 2.0 * shear_modulus * strain_yy, lame_lambda * trace + 2.0 * shear_modulus * strain_zz, 2.0 * shear_modulus * strain_xy, 2.0 * shear_modulus * strain_xz, 2.0 * shear_modulus * strain_yz])
    memory = RELAX * memory + (1.0 - RELAX) * relaxation * elastic
    stress = stress + TIME_STEP * (elastic - memory)
    return (velocity, stress, memory)

def reference(velocity, stress, memory, buoyancy, lame_lambda, shear_modulus, relaxation, surface_history, site_owner, periods):
    samples = []
    for step in range(ITERS):
        velocity, stress, memory = wave_step(velocity, stress, memory, buoyancy, lame_lambda, shear_modulus, relaxation)
        samples.append(velocity[:, :, :, 0].astype(jnp.bfloat16))
    fresh = jnp.transpose(jnp.stack(samples), (2, 3, 1, 0))
    window = jnp.concatenate([surface_history, fresh], axis=3)
    width = HIST + ITERS
    table = oscillator_table(periods, HIST, ITERS)
    owners = jnp.transpose(site_owner[..., 0], (0, 2, 1, 3)).reshape(N_GX, CX, NY)
    window_rows = window.reshape(N_GX, CX, NY, 3, width)

    def row_energy(item):
        rows_window, rows_owner = item
        response = jnp.dot(rows_window.reshape(-1, width), table, preferred_element_type=jnp.float32)
        power = (response * response).reshape(CX * NY, 3 * ITERS * P_SIZE)
        onehot = (rows_owner.reshape(-1)[:, None] == jnp.arange(N_GY, dtype=jnp.int32)[None, :]).astype(jnp.float32)
        return jnp.dot(onehot.T, power, precision=lax.Precision.HIGHEST) / SITES
    energy = lax.map(row_energy, (window_rows, owners))
    return (velocity, stress, memory, energy.reshape(N_GX, N_GY, 3, ITERS * P_SIZE))
```

```python
import functools
import math

import jax
import jax.numpy as jnp
from jax import lax
from jax.experimental import pallas as pl
from jax.experimental.pallas import tpu as pltpu
from jax.sharding import PartitionSpec as P

ITERS = 4
TIME_STEP = 0.25
DAMPING = 0.05
RELAX = math.exp(-0.25 / 8.0)
MESH = pl.DeviceIdType.MESH

ROWS = 96
NEAR = (0, 1, 2, 3, 4, 5, 6, 7, 8)
FAR_X = (0, 3, 4)
FAR_Y = (1, 3, 5)
WAYS = ((-1, 0), (1, 0), (0, -1), (0, 1), (-1, -1), (-1, 1), (1, -1), (1, 1))


def kernel(
    nx, ny, count_p,
    v_in, s_in, m_in, b_in, l_in, g_in, r_in, hist, owner, per,
    v_out, s_out, m_out, e_out,
    ext, bext, mem, coef, xs, xr, ys, yr, cs, cr, hi, lo, table, acc, fresh, msg, got,
    send_sem, recv_sem, esend_sem, erecv_sem,
):
    ix = lax.axis_index("gx")
    iy = lax.axis_index("gy")

    def exists(dx, dy):
        ok = None
        for at, d, n in ((ix, dx, nx), (iy, dy, ny)):
            if d:
                one = at + d >= 0 if d < 0 else at + d < n
                ok = one if ok is None else jnp.logical_and(ok, one)
        return ok

    barrier = pltpu.get_barrier_semaphore()
    total = ny - 1
    for dx, dy in WAYS:
        if dx:
            here = exists(dx, dy)
            total = total + here.astype(jnp.int32)

            @pl.when(here)
            def _():
                pl.semaphore_signal(barrier, inc=1, device_id=(ix + dx, iy + dy), device_id_type=MESH)

    def greet(i, carry):
        pl.semaphore_signal(barrier, inc=1, device_id=(ix, lax.rem(iy + i, ny)), device_id_type=MESH)
        return carry

    lax.fori_loop(1, ny, greet, 0)

    ext[...] = jnp.zeros_like(ext)
    bext[...] = jnp.zeros_like(bext)
    mem[...] = jnp.zeros_like(mem)
    coef[...] = jnp.zeros_like(coef)
    fresh[...] = jnp.zeros_like(fresh)
    for y in range(4):
        for c in range(6):
            ext[pl.ds(c * ROWS + 18 + y, 8, stride=8), :] = s_in[pl.ds(c * 32 + y, 8, stride=4), :]
        for c in range(3):
            ext[pl.ds((6 + c) * ROWS + 18 + y, 8, stride=8), :] = v_in[pl.ds(c * 32 + y, 8, stride=4), :]
        bext[pl.ds(18 + y, 8, stride=8), :] = b_in[pl.ds(y, 8, stride=4), :]

    def copy_of(step, way):
        dx, dy = WAYS[way]
        if dx and dy:
            src, dst = cs.at[step, way - 4], cr.at[step, way - 4]
        elif dx:
            src, dst = xs.at[step, way], xr.at[step, way]
        else:
            src, dst = ys.at[step, way - 2], yr.at[step, way - 2]
        if not (dx and dy) and step > 0:
            src, dst = src.at[pl.ds(0, 12)], dst.at[pl.ds(0, 12)]
        return pltpu.make_async_remote_copy(
            src_ref=src, dst_ref=dst,
            send_sem=send_sem.at[step, way], recv_sem=recv_sem.at[step, way],
            device_id=(ix + dx, iy + dy), device_id_type=MESH,
        )

    def pack(step):
        for way, (dx, dy) in enumerate(WAYS):
            if dx and dy:
                cell = (2 if dx < 0 else 9) * 8 + (2 if dy < 0 else 5)
                cs[step, way - 4] = ext[pl.ds(cell, 8, stride=ROWS), :]
            elif dx:
                near, far = (2, 3) if dx < 0 else (9, 8)
                for k, c in enumerate(NEAR):
                    xs[step, way, k] = ext[c * ROWS + near * 8:c * ROWS + near * 8 + 8, :]
                for k, c in enumerate(FAR_X):
                    xs[step, way, 9 + k] = ext[c * ROWS + far * 8:c * ROWS + far * 8 + 8, :]
                if step == 0:
                    xs[step, way, 12] = bext[near * 8:near * 8 + 8, :]
            else:
                near, far = (2, 3) if dy < 0 else (5, 4)
                for k, c in enumerate(NEAR):
                    ys[step, way - 2, k] = ext[pl.ds(c * ROWS + 16 + near, 8, stride=8), :]
                for k, c in enumerate(FAR_Y):
                    ys[step, way - 2, 9 + k] = ext[pl.ds(c * ROWS + 16 + far, 8, stride=8), :]
                if step == 0:
                    ys[step, way - 2, 12] = bext[pl.ds(16 + near, 8, stride=8), :]

    def start(step):
        for way in (4, 5, 6, 7, 2, 3, 0, 1):
            @pl.when(exists(*WAYS[way]))
            def _():
                copy_of(step, way).start()

    def land(step):
        for way, (dx, dy) in enumerate(WAYS):
            @pl.when(exists(-dx, -dy))
            def _():
                copy_of(step, way).wait_recv()
                if dx and dy:
                    cell = (10 if dx < 0 else 1) * 8 + (6 if dy < 0 else 1)
                    ext[pl.ds(cell, 6, stride=ROWS), :] = cr[step, way - 4, 0:6, :]
                elif dx:
                    near, far = (10, 11) if dx < 0 else (1, 0)
                    for k, c in enumerate(NEAR):
                        ext[c * ROWS + near * 8:c * ROWS + near * 8 + 8, :] = xr[step, way, k]
                    for k, c in enumerate(FAR_X):
                        ext[c * ROWS + far * 8:c * ROWS + far * 8 + 8, :] = xr[step, way, 9 + k]
                    if step == 0:
                        bext[near * 8:near * 8 + 8, :] = xr[step, way, 12]
                else:
                    near, far = (6, 7) if dy < 0 else (1, 0)
                    for k, c in enumerate(NEAR):
                        ext[pl.ds(c * ROWS + 16 + near, 8, stride=8), :] = yr[step, way - 2, k]
                    for k, c in enumerate(FAR_Y):
                        ext[pl.ds(c * ROWS + 16 + far, 8, stride=8), :] = yr[step, way - 2, 9 + k]
                    if step == 0:
                        bext[pl.ds(16 + near, 8, stride=8), :] = yr[step, way - 2, 12]

    lane = lax.broadcasted_iota(jnp.int32, (1, 1, 128), 2)

    def diff_x(f):
        return f[2:] - f[:-2]

    def diff_y(f):
        return pltpu.roll(f, 7, 1) - pltpu.roll(f, 1, 1)

    def diff_z(f):
        above = jnp.where(lane == 127, 0.0, pltpu.roll(f, 127, 2))
        below = jnp.where(lane == 0, 0.0, pltpu.roll(f, 1, 2))
        return above - below

    def field(c, first, last):
        return ext[c * ROWS + first * 8:c * ROWS + last * 8, :].reshape(last - first, 8, 128)

    def move(step):
        s = [field(c, 0, 12) for c in range(6)]
        push = bext[8:88, :].reshape(10, 8, 128) * (0.5 * TIME_STEP)
        forces = (
            diff_x(s[0]) + diff_y(s[3][1:11]) + diff_z(s[4][1:11]),
            diff_x(s[3]) + diff_y(s[1][1:11]) + diff_z(s[5][1:11]),
            diff_x(s[4]) + diff_y(s[5][1:11]) + diff_z(s[2][1:11]),
        )
        for c in range(3):
            v = field(6 + c, 1, 11) + push * forces[c]
            ext[(6 + c) * ROWS + 8:(6 + c) * ROWS + 88, :] = v.reshape(80, 128)
            top = jnp.where(lane == 128 - ITERS + step, v[1:9, :, 0:1], 0.0).reshape(64, 128)
            fresh[c * 64:c * 64 + 64, :] = fresh[c * 64:c * 64 + 64, :] + top

    def strain(step):
        v = [field(6 + c, 1, 11) for c in range(3)]
        mid = [f[1:9] for f in v]
        lam, mu, rel = (coef[k].reshape(8, 8, 128) for k in range(3))
        xx, yy, zz = diff_x(v[0]) * 0.5, diff_y(mid[1]) * 0.5, diff_z(mid[2]) * 0.5
        trace = lam * (xx + yy + zz)
        twice = 2.0 * mu
        half = 0.5 * mu
        rates = (
            trace + twice * xx,
            trace + twice * yy,
            trace + twice * zz,
            half * (diff_y(mid[0]) + diff_x(v[1])),
            half * (diff_z(mid[0]) + diff_x(v[2])),
            half * (diff_z(mid[1]) + diff_y(mid[2])),
        )
        gain = (1.0 - RELAX) * rel
        for c in range(6):
            m = RELAX * mem[c].reshape(8, 8, 128) + gain * rates[c]
            mem[c] = m.reshape(64, 128)
            s = field(c, 2, 10) + TIME_STEP * (rates[c] - m)
            ext[c * ROWS + 16:c * ROWS + 80, :] = s.reshape(64, 128)

    span = hi.shape[2]
    q = lax.broadcasted_iota(jnp.int32, (1, span), 1)
    step_of = jnp.zeros((1, span), jnp.int32)
    for t in range(1, ITERS):
        step_of = step_of + (q >= t * count_p).astype(jnp.int32)
    width = table.shape[0]
    length = width - ITERS

    def powers():
        omega = (2.0 * math.pi) / per[...]
        damped = omega * math.sqrt(1.0 - DAMPING * DAMPING)
        row = lax.broadcasted_iota(jnp.int32, (32, span), 0)
        low = (31 - row).astype(jnp.float32)
        high = (length - 31 + step_of - 32 * row).astype(jnp.float32)
        size = jnp.exp(-DAMPING * omega * low)
        lo[0] = size * jnp.cos(damped * low)
        lo[1] = size * jnp.sin(damped * low)
        size = jnp.exp(-DAMPING * omega * high) * (omega / damped)
        hi[0] = size * jnp.sin(damped * high)
        hi[1] = size * jnp.cos(damped * high)

    def fill():
        def one(a, carry):
            value = hi[0, pl.ds(a, 1), :] * lo[0] + hi[1, pl.ds(a, 1), :] * lo[1]
            row = lax.broadcasted_iota(jnp.int32, (32, span), 0) + 32 * a
            lag = length + step_of - row
            valid = jnp.logical_and(lag >= 0, lag <= length)
            table[pl.ds(pl.multiple_of(a * 32, 32), 32), :] = jnp.where(valid, value, 0.0).astype(jnp.bfloat16)
            return carry

        lax.fori_loop(0, width // 32, one, 0)

    def history():
        acc[...] = jnp.dot(hist[...], table[...], preferred_element_type=jnp.float32)

    pack(0)
    pl.semaphore_wait(barrier, total)
    start(0)
    for y in range(4):
        for c in range(6):
            mem[c, pl.ds(2 + y, 8, stride=8), :] = m_in[pl.ds(c * 32 + y, 8, stride=4), :]
        for k, ref in enumerate((l_in, g_in, r_in)):
            coef[k, pl.ds(2 + y, 8, stride=8), :] = ref[pl.ds(y, 8, stride=4), :]
    powers()
    for step in range(ITERS):
        land(step)
        move(step)
        if step < ITERS - 1:
            strain(step)
            pack(step + 1)
            start(step + 1)
            if step == 0:
                fill()
            if step == 1:
                history()

    rows = [fresh[pl.ds(c * 64 + 2 + y, 8, stride=8), :] for c in range(3) for y in range(4)]
    recent = jnp.concatenate(rows, axis=0).astype(jnp.bfloat16)
    response = acc[...] + jnp.dot(recent, table[width - 128:, :], preferred_element_type=jnp.float32)
    power = response * response
    sites = owner.shape[1]
    flat = jnp.concatenate([power[c * sites:(c + 1) * sites] for c in range(3)], axis=1)
    onehot = jnp.where(lax.broadcasted_iota(jnp.int32, (ny, sites), 0) == owner[...], 1.0, 0.0)
    sums = jnp.dot(onehot, flat, precision=lax.Precision.HIGHEST, preferred_element_type=jnp.float32) * (1.0 / sites)
    for o in range(ny):
        msg[o] = sums[o:o + 1, :]

    def energy_copy(i):
        to = lax.rem(iy + i, ny)
        return pltpu.make_async_remote_copy(
            src_ref=msg.at[to], dst_ref=got.at[i],
            send_sem=esend_sem.at[i], recv_sem=erecv_sem.at[i],
            device_id=(ix, to), device_id_type=MESH,
        )

    def send_energy(i, carry):
        energy_copy(i).start()
        return carry

    lax.fori_loop(1, ny, send_energy, 0)

    strain(ITERS - 1)
    for y in range(4):
        for c in range(6):
            s_out[pl.ds(c * 32 + y, 8, stride=4), :] = ext[pl.ds(c * ROWS + 18 + y, 8, stride=8), :]
            m_out[pl.ds(c * 32 + y, 8, stride=4), :] = mem[c, pl.ds(2 + y, 8, stride=8), :]
        for c in range(3):
            v_out[pl.ds(c * 32 + y, 8, stride=4), :] = ext[pl.ds((6 + c) * ROWS + 18 + y, 8, stride=8), :]
    for step in range(ITERS):
        for way in range(8):
            @pl.when(exists(*WAYS[way]))
            def _():
                copy_of(step, way).wait_send()

    def take(i, energy):
        energy_copy(i).wait()
        return energy + got[i]

    energy = lax.fori_loop(1, ny, take, msg[iy])
    for c in range(3):
        e_out[c:c + 1, :] = energy[:, c * span:c * span + e_out.shape[1]]


def solution(mesh):
    nx, ny = mesh.shape["gx"], mesh.shape["gy"]

    def on_device(velocity, stress, memory, buoyancy, lame_lambda, shear_modulus, relaxation,
                  surface_history, site_owner, periods):
        _, cx, cy, cz = velocity.shape
        sites = cx * cy
        length = surface_history.shape[3]
        width = length + ITERS
        count_p = periods.shape[0]
        cols = ITERS * count_p
        span = -(-cols // 128) * 128
        hist = jnp.transpose(surface_history, (2, 1, 0, 3)).reshape(3 * sites, length)
        hist = jnp.pad(hist, ((0, 0), (0, ITERS)))
        owner = jnp.transpose(site_owner.reshape(cx, cy)).reshape(1, sites)
        per = jnp.pad(jnp.tile(periods, ITERS), (0, span - cols), constant_values=3.0)[None, :]
        f32 = jnp.float32
        vmem = pl.BlockSpec(memory_space=pltpu.VMEM)
        out = pl.pallas_call(
            functools.partial(kernel, nx, ny, count_p),
            out_shape=(
                jax.ShapeDtypeStruct((3 * sites, cz), f32),
                jax.ShapeDtypeStruct((6 * sites, cz), f32),
                jax.ShapeDtypeStruct((6 * sites, cz), f32),
                jax.ShapeDtypeStruct((3, cols), f32),
            ),
            in_specs=[vmem] * 10,
            out_specs=(vmem,) * 4,
            scratch_shapes=[
                pltpu.VMEM((9 * ROWS, cz), f32),
                pltpu.VMEM((ROWS, cz), f32),
                pltpu.VMEM((6, 64, cz), f32),
                pltpu.VMEM((3, 64, cz), f32),
                pltpu.VMEM((ITERS, 2, 13, 8, cz), f32),
                pltpu.VMEM((ITERS, 2, 13, 8, cz), f32),
                pltpu.VMEM((ITERS, 2, 13, 8, cz), f32),
                pltpu.VMEM((ITERS, 2, 13, 8, cz), f32),
                pltpu.VMEM((ITERS, 4, 8, cz), f32),
                pltpu.VMEM((ITERS, 4, 8, cz), f32),
                pltpu.VMEM((2, 32, span), f32),
                pltpu.VMEM((2, 32, span), f32),
                pltpu.VMEM((width, span), jnp.bfloat16),
                pltpu.VMEM((3 * sites, span), f32),
                pltpu.VMEM((3 * 64, cz), f32),
                pltpu.VMEM((ny, 1, 3 * span), f32),
                pltpu.VMEM((ny, 1, 3 * span), f32),
                pltpu.SemaphoreType.DMA((ITERS, 8)),
                pltpu.SemaphoreType.DMA((ITERS, 8)),
                pltpu.SemaphoreType.DMA((ny,)),
                pltpu.SemaphoreType.DMA((ny,)),
            ],
            compiler_params=pltpu.CompilerParams(
                collective_id=0, has_side_effects=True, vmem_limit_bytes=32 * 1024 * 1024
            ),
        )(
            velocity.reshape(3 * sites, cz), stress.reshape(6 * sites, cz), memory.reshape(6 * sites, cz),
            buoyancy.reshape(sites, cz), lame_lambda.reshape(sites, cz), shear_modulus.reshape(sites, cz),
            relaxation.reshape(sites, cz), hist, owner, per,
        )
        return (
            out[0].reshape(3, cx, cy, cz), out[1].reshape(6, cx, cy, cz), out[2].reshape(6, cx, cy, cz),
            out[3].reshape(1, 1, 3, cols),
        )

    field4 = P(None, "gx", "gy", None)
    field3 = P("gx", "gy", None)
    return jax.shard_map(
        on_device, mesh=mesh,
        in_specs=(field4, field4, field4, field3, field3, field3, field3,
                  P("gx", "gy", None, None), P("gx", "gy", None, None, None), P()),
        out_specs=(field4, field4, field4, P("gx", "gy", None, None)),
        check_vma=False,
    )
```

```python
import functools
import math

import jax
import jax.numpy as jnp
from jax import lax
from jax.experimental import pallas as pl
from jax.experimental.pallas import tpu as pltpu
from jax.sharding import PartitionSpec as P

ITERS = 4
TIME_STEP = 0.25
DAMPING = 0.05
RELAX = math.exp(-0.25 / 8.0)
MESH = pl.DeviceIdType.MESH

ROWS = 96
BY_X = (0, 3, 4)
BY_Y = (3, 1, 5)
BY_Z = (4, 5, 2)
WAYS = ((-1, 0), (1, 0), (0, -1), (0, 1), (-1, -1), (-1, 1), (1, -1), (1, 1))


def kernel(
    nx, ny, count_p,
    v_hbm, s_hbm, m_hbm, b_hbm, l_hbm, g_hbm, r_hbm, hist_hbm, owner_hbm, per_hbm,
    v_out, s_out, m_out, e_out,
    v_in, s_in, m_in, b_in, l_in, g_in, r_in, hist_in, owner, per_in,
    ext, bext, mem, coef, xs, xr, ys, yr, cs, cr, hist, per, hi, lo, table, acc, fresh, late, msg, got,
    load_sem, send_sem, recv_sem, esend_sem, erecv_sem,
):
    ix = lax.axis_index("gx")
    iy = lax.axis_index("gy")

    def exists(dx, dy):
        ok = None
        for at, d, n in ((ix, dx, nx), (iy, dy, ny)):
            if d:
                one = at + d >= 0 if d < 0 else at + d < n
                ok = one if ok is None else jnp.logical_and(ok, one)
        return ok

    loads = [
        pltpu.make_async_copy(src, dst, load_sem.at[i])
        for i, (src, dst) in enumerate((
            (s_hbm, s_in), (v_hbm, v_in), (b_hbm, b_in), (m_hbm, m_in), (l_hbm, l_in),
            (g_hbm, g_in), (r_hbm, r_in), (per_hbm, per_in), (hist_hbm, hist_in), (owner_hbm, owner),
        ))
    ]
    for load in loads:
        load.start()

    for buf in (xr, yr, cr):
        buf[...] = jnp.zeros_like(buf)

    barrier = pltpu.get_barrier_semaphore()
    total = ny - 1
    for dx, dy in WAYS:
        if dx:
            here = exists(dx, dy)
            total = total + here.astype(jnp.int32)

            @pl.when(here)
            def _():
                pl.semaphore_signal(barrier, inc=1, device_id=(ix + dx, iy + dy), device_id_type=MESH)

    def greet(i, carry):
        pl.semaphore_signal(barrier, inc=1, device_id=(ix, lax.rem(iy + i, ny)), device_id_type=MESH)
        return carry

    lax.fori_loop(1, ny, greet, 0)

    ext[...] = jnp.zeros_like(ext)
    bext[...] = jnp.zeros_like(bext)
    mem[...] = jnp.zeros_like(mem)
    coef[...] = jnp.zeros_like(coef)
    fresh[...] = jnp.zeros_like(fresh)
    for load in loads[:3]:
        load.wait()
    for y in range(4):
        for c in range(6):
            ext[pl.ds(c * ROWS + 18 + y, 8, stride=8), :] = s_in[pl.ds(c * 32 + y, 8, stride=4), :]
        for c in range(3):
            ext[pl.ds((6 + c) * ROWS + 18 + y, 8, stride=8), :] = v_in[pl.ds(c * 32 + y, 8, stride=4), :]
        bext[pl.ds(18 + y, 8, stride=8), :] = b_in[pl.ds(y, 8, stride=4), :]

    def copy_of(step, way):
        dx, dy = WAYS[way]
        if dx and dy:
            src, dst = cs.at[step, way - 4], cr.at[step, way - 4]
        elif dx:
            src, dst = xs.at[step, way], xr.at[step, way]
        else:
            src, dst = ys.at[step, way - 2], yr.at[step, way - 2]
        if not (dx and dy) and step > 0:
            count = 3 if dx else 6
            src, dst = src.at[pl.ds(0, count)], dst.at[pl.ds(0, count)]
        return pltpu.make_async_remote_copy(
            src_ref=src, dst_ref=dst,
            send_sem=send_sem.at[step, way], recv_sem=recv_sem.at[step, way],
            device_id=(ix + dx, iy + dy), device_id_type=MESH,
        )

    lane = lax.broadcasted_iota(jnp.int32, (1, 128), 1)
    sub = lax.broadcasted_iota(jnp.int32, (8, 1), 0)
    push_by = 0.5 * TIME_STEP

    def diff_z(f):
        axis = f.ndim - 1
        above = jnp.where(lane == 127, 0.0, pltpu.roll(f, 127, axis))
        below = jnp.where(lane == 0, 0.0, pltpu.roll(f, 1, axis))
        return above - below

    def x_tile(c, x):
        return ext[c * ROWS + (x + 2) * 8:c * ROWS + (x + 2) * 8 + 8, :]

    def y_tile(c, y):
        return ext[pl.ds(c * ROWS + 18 + y, 8, stride=8), :]

    def inside(f, first, last):
        above = jnp.where(sub == last, 0.0, pltpu.roll(f, 7, 0))
        below = jnp.where(sub == first, 0.0, pltpu.roll(f, 1, 0))
        return above - below

    def pack(step):
        for way, (dx, dy) in enumerate(WAYS):
            if dx and dy:
                cell = (2 if dx < 0 else 9) * 8 + (2 if dy < 0 else 5)
                cs[step, way - 4] = ext[pl.ds(cell, 8, stride=ROWS), :]
            elif dx:
                near, far, sign = (0, 1, 1.0) if dx < 0 else (7, 6, -1.0)
                push = bext[(near + 2) * 8:(near + 2) * 8 + 8, :]
                keep = jnp.logical_and(sub >= 2, sub < 6)
                for c in range(3):
                    force = sign * x_tile(BY_X[c], far) + inside(x_tile(BY_Y[c], near), 2, 5) + diff_z(x_tile(BY_Z[c], near))
                    v = x_tile(6 + c, near) + (push_by * push) * force
                    xs[step, way, c] = jnp.where(keep, x_tile(BY_X[c], near), pltpu.roll(v, 4, 0))
                if step == 0:
                    xs[step, way, 3] = push
            else:
                near, far, sign = (0, 1, 1.0) if dy < 0 else (3, 2, -1.0)
                push = bext[pl.ds(18 + near, 8, stride=8), :]
                for c in range(3):
                    force = inside(y_tile(BY_X[c], near), 0, 7) + sign * y_tile(BY_Y[c], far) + diff_z(y_tile(BY_Z[c], near))
                    ys[step, way - 2, c] = y_tile(BY_Y[c], near)
                    ys[step, way - 2, 3 + c] = y_tile(6 + c, near) + (push_by * push) * force
                if step == 0:
                    ys[step, way - 2, 6] = push

    def start(step):
        for way in (4, 5, 6, 7, 2, 3, 0, 1):
            @pl.when(exists(*WAYS[way]))
            def _():
                copy_of(step, way).start()

    def land(step):
        for way, (dx, dy) in enumerate(WAYS):
            @pl.when(exists(-dx, -dy))
            def _():
                copy_of(step, way).wait_recv()

        for way, (dx, dy) in enumerate(WAYS[:4]):
            if dx:
                out, near, sign = (8, 7, -1.0) if dx < 0 else (-1, 0, 1.0)
                push = xr[0, way, 3] * push_by
                low, high = WAYS.index((dx, 1)) - 4, WAYS.index((dx, -1)) - 4
                for c in range(3):
                    both = xr[step, way, c]
                    corner = jnp.where(sub == 2, -cr[step, low, BY_Y[c]:BY_Y[c] + 1, :], 0.0)
                    corner = corner + jnp.where(sub == 5, cr[step, high, BY_Y[c]:BY_Y[c] + 1, :], 0.0)
                    v = pltpu.roll(both, 4, 0) + push * (corner + sign * x_tile(BY_X[c], near))
                    at = (out + 2) * 8
                    ext[BY_X[c] * ROWS + at:BY_X[c] * ROWS + at + 8, :] = both
                    ext[(6 + c) * ROWS + at:(6 + c) * ROWS + at + 8, :] = v
            else:
                out, near, sign = (4, 3, -1.0) if dy < 0 else (-1, 0, 1.0)
                push = yr[0, way - 2, 6] * push_by
                low, high = WAYS.index((1, dy)) - 4, WAYS.index((-1, dy)) - 4
                for c in range(3):
                    corner = jnp.where(sub == 0, -cr[step, low, BY_X[c]:BY_X[c] + 1, :], 0.0)
                    corner = corner + jnp.where(sub == 7, cr[step, high, BY_X[c]:BY_X[c] + 1, :], 0.0)
                    v = yr[step, way - 2, 3 + c] + push * (corner + sign * y_tile(BY_Y[c], near))
                    ext[pl.ds(BY_Y[c] * ROWS + 18 + out, 8, stride=8), :] = yr[step, way - 2, c]
                    ext[pl.ds((6 + c) * ROWS + 18 + out, 8, stride=8), :] = v

    def diff_x(f):
        return f[2:] - f[:-2]

    def diff_y(f):
        return pltpu.roll(f, 7, 1) - pltpu.roll(f, 1, 1)

    def field(c, first, last):
        return ext[c * ROWS + first * 8:c * ROWS + last * 8, :].reshape(last - first, 8, 128)

    def move(step):
        s = [field(c, 1, 11) for c in range(6)]
        push = bext[16:80, :].reshape(8, 8, 128) * push_by
        inner = jnp.logical_and(sub >= 2, sub < 6)
        for c in range(3):
            force = diff_x(s[BY_X[c]]) + diff_y(s[BY_Y[c]][1:9]) + diff_z(s[BY_Z[c]][1:9])
            old = field(6 + c, 2, 10)
            v = jnp.where(inner, old + push * force, old)
            ext[(6 + c) * ROWS + 16:(6 + c) * ROWS + 80, :] = v.reshape(64, 128)
            top = jnp.where(lane == 128 - ITERS + step, v[:, :, 0:1], 0.0).reshape(64, 128)
            fresh[c * 64:c * 64 + 64, :] = fresh[c * 64:c * 64 + 64, :] + top

    def strain(step):
        v = [field(6 + c, 1, 11) for c in range(3)]
        mid = [f[1:9] for f in v]
        lam, mu, rel = (coef[k].reshape(8, 8, 128) for k in range(3))
        xx, yy, zz = diff_x(v[0]) * 0.5, diff_y(mid[1]) * 0.5, diff_z(mid[2]) * 0.5
        trace = lam * (xx + yy + zz)
        twice = 2.0 * mu
        half = 0.5 * mu
        rates = (
            trace + twice * xx,
            trace + twice * yy,
            trace + twice * zz,
            half * (diff_y(mid[0]) + diff_x(v[1])),
            half * (diff_z(mid[0]) + diff_x(v[2])),
            half * (diff_z(mid[1]) + diff_y(mid[2])),
        )
        gain = (1.0 - RELAX) * rel
        for c in range(6):
            m = RELAX * mem[c].reshape(8, 8, 128) + gain * rates[c]
            mem[c] = m.reshape(64, 128)
            s = field(c, 2, 10) + TIME_STEP * (rates[c] - m)
            ext[c * ROWS + 16:c * ROWS + 80, :] = s.reshape(64, 128)

    span = hi.shape[2]
    q = lax.broadcasted_iota(jnp.int32, (1, span), 1)
    step_of = jnp.zeros((1, span), jnp.int32)
    for t in range(1, ITERS):
        step_of = step_of + (q >= t * count_p).astype(jnp.int32)
    width = table.shape[0]
    length = width - ITERS

    def prepare():
        cols = per_in.shape[1]
        per[...] = jnp.full_like(per, 3.0)
        for t in range(ITERS):
            per[:, t * cols:(t + 1) * cols] = per_in[...]
        hist[:, width - 128:] = jnp.zeros((hist.shape[0], 128), jnp.float32)
        for x in range(8):
            for c in range(3):
                at = c * 32 + x * 4
                hist[at:at + 4, 0:length] = hist_in[x, c].astype(jnp.float32)

    def powers():
        omega = (2.0 * math.pi) / per[...]
        damped = omega * math.sqrt(1.0 - DAMPING * DAMPING)
        row = lax.broadcasted_iota(jnp.int32, (32, span), 0)
        low = (31 - row).astype(jnp.float32)
        high = (length - 31 + step_of - 32 * row).astype(jnp.float32)
        size = jnp.exp(-DAMPING * omega * low)
        lo[0] = size * jnp.cos(damped * low)
        lo[1] = size * jnp.sin(damped * low)
        size = jnp.exp(-DAMPING * omega * high) * (omega / damped)
        hi[0] = size * jnp.sin(damped * high)
        hi[1] = size * jnp.cos(damped * high)

    def fill():
        def one(a, carry):
            value = hi[0, pl.ds(a, 1), :] * lo[0] + hi[1, pl.ds(a, 1), :] * lo[1]
            row = lax.broadcasted_iota(jnp.int32, (32, span), 0) + 32 * a
            lag = length + step_of - row
            valid = jnp.logical_and(lag >= 0, lag <= length)
            table[pl.ds(pl.multiple_of(a * 32, 32), 32), :] = jnp.where(valid, value, 0.0).astype(jnp.bfloat16)
            return carry

        lax.fori_loop(0, width // 32, one, 0)

    def history():
        acc[...] = jnp.dot(hist[...].astype(jnp.bfloat16), table[...], preferred_element_type=jnp.float32)

    pack(0)
    pl.semaphore_wait(barrier, total)
    start(0)
    for load in loads[3:]:
        load.wait()
    for y in range(4):
        for c in range(6):
            mem[c, pl.ds(2 + y, 8, stride=8), :] = m_in[pl.ds(c * 32 + y, 8, stride=4), :]
        for k, ref in enumerate((l_in, g_in, r_in)):
            coef[k, pl.ds(2 + y, 8, stride=8), :] = ref[pl.ds(y, 8, stride=4), :]
    prepare()
    powers()
    for step in range(ITERS):
        land(step)
        move(step)
        if step < ITERS - 1:
            strain(step)
            pack(step + 1)
            start(step + 1)
            if step == 0:
                fill()
            if step == 1:
                history()

    for c in range(3):
        for y in range(4):
            late[pl.ds(c * 32 + y, 8, stride=4), :] = fresh[pl.ds(c * 64 + 2 + y, 8, stride=8), :]
    recent = late[...].astype(jnp.bfloat16)
    response = acc[...] + jnp.dot(recent, table[width - 128:, :], preferred_element_type=jnp.float32)
    power = response * response
    sites = owner.shape[0] * owner.shape[1]
    flat = jnp.concatenate([power[c * sites:(c + 1) * sites] for c in range(3)], axis=1)
    at_x = lax.broadcasted_iota(jnp.int32, (8, sites), 1) // 4 == lax.broadcasted_iota(jnp.int32, (8, sites), 0)
    at_y = lax.broadcasted_iota(jnp.int32, (4, sites), 1) % 4 == lax.broadcasted_iota(jnp.int32, (4, sites), 0)
    spread = jnp.dot(owner[...].astype(jnp.float32), jnp.where(at_x, 1.0, 0.0),
                     precision=lax.Precision.HIGHEST, preferred_element_type=jnp.float32)
    named = jnp.sum(jnp.where(at_y, spread, 0.0), axis=0, keepdims=True)
    block = lax.broadcasted_iota(jnp.int32, (ny, sites), 0).astype(jnp.float32)
    onehot = jnp.where(block == named, 1.0, 0.0)
    sums = jnp.dot(onehot, flat, precision=lax.Precision.HIGHEST, preferred_element_type=jnp.float32) * (1.0 / sites)
    for o in range(ny):
        msg[o] = sums[o:o + 1, :]

    def energy_copy(i):
        to = lax.rem(iy + i, ny)
        return pltpu.make_async_remote_copy(
            src_ref=msg.at[to], dst_ref=got.at[i],
            send_sem=esend_sem.at[i], recv_sem=erecv_sem.at[i],
            device_id=(ix, to), device_id_type=MESH,
        )

    def send_energy(i, carry):
        energy_copy(i).start()
        return carry

    lax.fori_loop(1, ny, send_energy, 0)

    strain(ITERS - 1)
    for y in range(4):
        for c in range(6):
            s_out[pl.ds(c * 32 + y, 8, stride=4), :] = ext[pl.ds(c * ROWS + 18 + y, 8, stride=8), :]
            m_out[pl.ds(c * 32 + y, 8, stride=4), :] = mem[c, pl.ds(2 + y, 8, stride=8), :]
        for c in range(3):
            v_out[pl.ds(c * 32 + y, 8, stride=4), :] = ext[pl.ds((6 + c) * ROWS + 18 + y, 8, stride=8), :]
    for step in range(ITERS):
        for way in range(8):
            @pl.when(exists(*WAYS[way]))
            def _():
                copy_of(step, way).wait_send()

    def take(i, energy):
        energy_copy(i).wait()
        return energy + got[i]

    energy = lax.fori_loop(1, ny, take, msg[iy])
    for c in range(3):
        e_out[c] = energy[:, c * span:c * span + e_out.shape[2]]


def place(*refs):
    ins, outs, held, sem = refs[:4], refs[4:8], refs[8:12], refs[12]
    fetch = [pltpu.make_async_copy(ins[i], held[i], sem.at[0, i]) for i in range(4)]
    store = [pltpu.make_async_copy(held[i], outs[i], sem.at[1, i]) for i in range(4)]
    for copy in fetch:
        copy.start()
    for i in range(4):
        fetch[i].wait()
        store[i].start()
    for copy in store:
        copy.wait()


def solution(mesh):
    nx, ny = mesh.shape["gx"], mesh.shape["gy"]

    def on_device(velocity, stress, memory, buoyancy, lame_lambda, shear_modulus, relaxation,
                  surface_history, site_owner, periods):
        _, cx, cy, cz = velocity.shape
        sites = cx * cy
        length = surface_history.shape[3]
        width = length + ITERS
        count_p = periods.shape[0]
        cols = ITERS * count_p
        span = -(-cols // 128) * 128
        hist = jnp.transpose(surface_history, (0, 2, 1, 3))
        owner = jnp.transpose(site_owner.reshape(cx, cy))
        f32 = jnp.float32
        vmem = pl.BlockSpec(memory_space=pltpu.VMEM)
        out = pl.pallas_call(
            functools.partial(kernel, nx, ny, count_p),
            out_shape=(
                jax.ShapeDtypeStruct((3 * sites, cz), f32),
                jax.ShapeDtypeStruct((6 * sites, cz), f32),
                jax.ShapeDtypeStruct((6 * sites, cz), f32),
                jax.ShapeDtypeStruct((3, 1, cols), f32),
            ),
            in_specs=[pl.BlockSpec(memory_space=pltpu.HBM)] * 10,
            out_specs=(vmem,) * 4,
            scratch_shapes=[
                pltpu.VMEM((3 * sites, cz), f32),
                pltpu.VMEM((6 * sites, cz), f32),
                pltpu.VMEM((6 * sites, cz), f32),
                pltpu.VMEM((sites, cz), f32),
                pltpu.VMEM((sites, cz), f32),
                pltpu.VMEM((sites, cz), f32),
                pltpu.VMEM((sites, cz), f32),
                pltpu.VMEM((cx, 3, cy, length), jnp.bfloat16),
                pltpu.VMEM((cy, cx), jnp.int32),
                pltpu.VMEM((1, count_p), f32),
                pltpu.VMEM((9 * ROWS, cz), f32),
                pltpu.VMEM((ROWS, cz), f32),
                pltpu.VMEM((6, 64, cz), f32),
                pltpu.VMEM((3, 64, cz), f32),
                pltpu.VMEM((ITERS, 2, 4, 8, cz), f32),
                pltpu.VMEM((ITERS, 2, 4, 8, cz), f32),
                pltpu.VMEM((ITERS, 2, 7, 8, cz), f32),
                pltpu.VMEM((ITERS, 2, 7, 8, cz), f32),
                pltpu.VMEM((ITERS, 4, 8, cz), f32),
                pltpu.VMEM((ITERS, 4, 8, cz), f32),
                pltpu.VMEM((3 * sites, width), f32),
                pltpu.VMEM((1, span), f32),
                pltpu.VMEM((2, 32, span), f32),
                pltpu.VMEM((2, 32, span), f32),
                pltpu.VMEM((width, span), jnp.bfloat16),
                pltpu.VMEM((3 * sites, span), f32),
                pltpu.VMEM((3 * 64, cz), f32),
                pltpu.VMEM((3 * sites, cz), f32),
                pltpu.VMEM((ny, 1, 3 * span), f32),
                pltpu.VMEM((ny, 1, 3 * span), f32),
                pltpu.SemaphoreType.DMA((10,)),
                pltpu.SemaphoreType.DMA((ITERS, 8)),
                pltpu.SemaphoreType.DMA((ITERS, 8)),
                pltpu.SemaphoreType.DMA((ny,)),
                pltpu.SemaphoreType.DMA((ny,)),
            ],
            compiler_params=pltpu.CompilerParams(
                collective_id=0, has_side_effects=True, vmem_limit_bytes=60 * 1024 * 1024
            ),
        )(
            velocity.reshape(3 * sites, cz), stress.reshape(6 * sites, cz), memory.reshape(6 * sites, cz),
            buoyancy.reshape(sites, cz), lame_lambda.reshape(sites, cz), shear_modulus.reshape(sites, cz),
            relaxation.reshape(sites, cz), hist, owner, periods[None, :],
        )
        out = pl.pallas_call(
            place,
            out_shape=tuple(jax.ShapeDtypeStruct(part.shape, part.dtype) for part in out),
            in_specs=[pl.BlockSpec(memory_space=pl.ANY)] * 4,
            out_specs=(pl.BlockSpec(memory_space=pltpu.HBM),) * 4,
            scratch_shapes=[pltpu.VMEM(part.shape, part.dtype) for part in out] + [pltpu.SemaphoreType.DMA((2, 4))],
            compiler_params=pltpu.CompilerParams(vmem_limit_bytes=60 * 1024 * 1024),
        )(*out)
        return (
            out[0].reshape(3, cx, cy, cz), out[1].reshape(6, cx, cy, cz), out[2].reshape(6, cx, cy, cz),
            jnp.transpose(out[3], (1, 0, 2))[None],
        )

    field4 = P(None, "gx", "gy", None)
    field3 = P("gx", "gy", None)
    return jax.shard_map(
        on_device, mesh=mesh,
        in_specs=(field4, field4, field4, field3, field3, field3, field3,
                  P("gx", "gy", None, None), P("gx", "gy", None, None, None), P()),
        out_specs=(field4, field4, field4, P("gx", "gy", None, None)),
        check_vma=False,
    )
```
